32 devices in a mesh: pos: 8 (over z, x), grp: 4 (over y, core).
Axes of the slice: x: 2, y: 2, z: 4, core: 2. Of those that a mesh axis runs over, the one named last changes fastest.
Arguments:
- key_cache: bfloat16 [32768, 2048], P(('grp', 'pos')), parts along dimension 0, may hold values from -60 to 60
- init_basis: float32 [8192, 256], P('grp'), parts along dimension 0, may hold values from -0.125 to 0.125
Outputs:
- basis_scaled: float32 [8192, 256], P('grp'), parts along dimension 0
- latents: bfloat16 [32768, 256], P(('grp', 'pos')), parts along dimension 0
The draws below stay inside these ranges and needn't reach their ends.
There are 4 independent parts, one for each index of `grp`. The reference program is written for one: setup_inputs(seed, part) draws one part's arguments, and reference() takes and returns one part's arrays. A program takes and returns all parts, laid end to end along the dimension named above; each array names one. Nothing has to cross between parts.
All inputs are finite; a program needn't handle non-finite values.
Results may differ from the reference program's by a relative error of at most 0.0095.
Values may be sent and summed in bfloat16 or wider, within the bound.
A program may use at most 64 MiB of HBM per device.

```python
import jax
import jax.numpy as jnp
from jax import lax

W = 2048
R = 256
ITERS = 3
TOK_DEV = 1024
TOKENS = 8192
N_POS = 8


def draw_key_cache(key, part):
    key = jax.random.fold_in(key, 11)
    first = jax.random.fold_in(key, 0)
    second = jax.random.fold_in(key, 1)
    third = jax.random.fold_in(key, 2)
    fifth = jax.random.fold_in(key, 4)
    base = jnp.clip(jax.random.normal(first, (TOKENS, W), jnp.float32), -4.0, 4.0)
    row_scale = jnp.exp(jax.random.uniform(second, (TOKENS, 1), jnp.float32, jnp.log(0.5), jnp.log(5.0)))
    ramp = jnp.sqrt(1.0 + 2.0 * jnp.arange(TOKENS, dtype=jnp.float32) / TOKENS).reshape(TOKENS, 1)
    column_scale = jnp.exp(jax.random.uniform(third, (1, W), jnp.float32, jnp.log(0.5), jnp.log(2.0)))
    block_count = TOKENS // TOK_DEV
    block_scale = jnp.exp(jax.random.uniform(fifth, (block_count, 1, W), jnp.float32, jnp.log(0.3), jnp.log(3.0)))
    values = base * row_scale * ramp * column_scale
    values = (values.reshape(block_count, TOK_DEV, W) * block_scale).reshape(TOKENS, W)
    values = jnp.clip(values, -60.0, 60.0)
    return values.astype(jnp.bfloat16)


def centred(stream_key, dims, spread, most, held_as=jnp.bfloat16):
    return jnp.clip(spread * jax.random.normal(stream_key, dims, jnp.float32), -most, most).astype(held_as)


def setup_inputs(seed: int = 0, part: int = 0) -> dict:
    splits = jax.random.split(jax.random.key(seed), 3)
    own_keys = jax.random.split(jax.random.fold_in(splits[2], part), 3)
    key_cache = draw_key_cache(jax.random.fold_in(jax.random.fold_in(splits[2], part), 71), part)
    init_basis = centred(own_keys[1], (W, R), W ** -0.5, 0.125, jnp.float32)
    return {"key_cache": key_cache, "init_basis": init_basis}


def orthonormal(summed):
    gram_matrix = jnp.dot(summed.T, summed, precision=lax.Precision.HIGHEST)
    factor = jnp.linalg.cholesky(gram_matrix)
    return jax.scipy.linalg.solve_triangular(factor, summed.T, lower=True).T

def reference(key_cache, init_basis):
    basis = init_basis
    for sweep in range(ITERS):
        rounded = basis.astype(jnp.bfloat16)
        projected = jnp.dot(key_cache.astype(jnp.float32), rounded.astype(jnp.float32), preferred_element_type=jnp.float32).astype(jnp.bfloat16)
        summed = lax.dot_general(key_cache.astype(jnp.float32), projected.astype(jnp.float32), (((0,), (0,)), ((), ())), preferred_element_type=jnp.float32)
        basis = orthonormal(summed)
    compressed = jnp.dot(key_cache.astype(jnp.float32), basis.astype(jnp.bfloat16).astype(jnp.float32), preferred_element_type=jnp.float32).astype(jnp.bfloat16)
    blocks = compressed.reshape(N_POS, N_POS, TOK_DEV // N_POS, R)
    latents = jnp.transpose(blocks, (1, 0, 2, 3)).reshape(TOKENS, R)
    return (jnp.sqrt(jnp.float32(W)) * basis, latents)
```

```python
import functools

import jax
import jax.numpy as jnp
from jax import lax
from jax.experimental import pallas as pl
from jax.experimental.pallas import tpu as pltpu
from jax.sharding import PartitionSpec as P

ITERS = 3
CW = 128
F32 = jnp.float32
BF16 = jnp.bfloat16
HIGH = lax.Precision.HIGHEST


def dot(a, b, ca=1, cb=0, precision=None):
    return lax.dot_general(
        a, b, (((ca,), (cb,)), ((), ())), precision=precision, preferred_element_type=F32
    )


def halves(a):
    high = a.astype(BF16)
    return high, (a - high.astype(F32)).astype(BF16)


def dot3(a, b, ca=1, cb=0):
    bh, bl = halves(b)
    if a.dtype == BF16:
        return dot(a, bh, ca, cb) + dot(a, bl, ca, cb)
    ah, al = halves(a)
    return dot(ah, bh, ca, cb) + (dot(ah, bl, ca, cb) + dot(al, bh, ca, cb))


def inverse_factor(a_ref):
    lane = lax.broadcasted_iota(jnp.int32, (8, CW), 1)
    sub = lax.broadcasted_iota(jnp.int32, (8, CW), 0)
    rows = lax.broadcasted_iota(jnp.int32, (CW, CW), 0)
    cols = lax.broadcasted_iota(jnp.int32, (CW, CW), 1)

    def step(k, carry):
        start = pl.multiple_of(k * 8, 8)
        x = a_ref[pl.ds(start, 8), :]
        d = pltpu.roll(x, lax.rem(CW - start, CW), 1)
        c = [jnp.broadcast_to(d[:, r : r + 1], (8, CW)) for r in range(8)]
        x = jnp.where(
            (lane >= start) & (lane < start + 8),
            jnp.where(lane == start + sub, 1.0, 0.0),
            x,
        )
        for r in range(8):
            p = lax.rsqrt(c[r][r : r + 1, :])
            row = x[r : r + 1, :] * p
            m = jnp.where(sub > r, c[r] * p, 0.0)
            x = jnp.where(sub == r, row, x - m * row)
            for t in range(r + 1, 8):
                c[t] = c[t] - m * (c[t][r : r + 1, :] * p)
        a_ref[pl.ds(start, 8), :] = x
        w = jnp.where(lane >= start + 8, x, 0.0).T
        a = a_ref[...]
        a = jnp.where((cols >= start) & (cols < start + 8) & (rows >= start + 8), 0.0, a)
        for r in range(8):
            a = a - w[:, r : r + 1] * x[r : r + 1, :]
        a_ref[...] = a
        return carry

    lax.fori_loop(0, CW // 8, step, 0)
    a_ref[...] = jnp.where(cols <= rows, a_ref[...], 0.0)


def kernel(
    n, ni, no, key_ref, init_ref, basis_ref, latent_ref,
    keyt, prod, raw, praw, fact, cross, sl, r1, sb, r2, sf, comp,
    s1s, s1r, s2s, s2r, g2s, g2r, g1s, g1r, fs, fr,
):
    tokens, width = key_ref.shape
    chunks = init_ref.shape[1] // CW
    part, sub, blk = width // ni, width // n, tokens // n
    me = lax.axis_index("pos")
    i, o = lax.rem(me, ni), lax.div(me, ni)

    def device(oo, ii):
        return {"pos": oo * ni + ii}

    def inner(d):
        return lax.rem(i + d, ni)

    def outer(e):
        return lax.rem(o + e, no)

    def rows_of(oo, ii):
        return pl.ds(pl.multiple_of(ii * part + oo * sub, sub), sub)

    def remote(src, dst, ssem, rsem, dev):
        return pltpu.make_async_remote_copy(
            src_ref=src, dst_ref=dst, send_sem=ssem, recv_sem=rsem,
            device_id=dev, device_id_type=pl.DeviceIdType.MESH,
        )

    barrier = pltpu.get_barrier_semaphore()
    for q in range(1, n):
        pl.semaphore_signal(
            barrier, inc=1, device_id={"pos": lax.rem(me + q, n)},
            device_id_type=pl.DeviceIdType.MESH,
        )

    sf[0, 0] = init_ref[:, :CW].astype(BF16)
    sf[0, 1] = init_ref[:, CW:].astype(BF16)
    tile = 256

    @pl.loop(0, tokens // tile)
    def _(s):
        rows = pl.ds(pl.multiple_of(s * tile, tile), tile)
        for c in range(chunks):
            prod[c, rows] = dot(key_ref[rows, :], sf[0, c]).astype(BF16)

    @pl.loop(0, width // tile)
    def _(s):
        rows = pl.ds(pl.multiple_of(s * tile, tile), tile)
        keyt[rows, :] = key_ref[:, rows].T

    pl.semaphore_wait(barrier, n - 1)

    sends = [[] for _ in range(chunks)]

    def send(c):
        for copy in sends[c]:
            copy.wait_send()
        sends[c] = []
        for e in list(range(1, no)) + [0]:
            for d in range(1, ni):
                rows = rows_of(outer(e), inner(d))
                sl[c, rows] = dot(keyt[rows, :], prod[c]).astype(BF16)
                copy = remote(
                    sl.at[c, rows], r1.at[c, d - 1, e], s1s.at[c, d - 1, e],
                    s1r.at[c, d - 1, e], device(o, inner(d)),
                )
                copy.start()
                sends[c].append(copy)

    def combine(c, buf):
        first = sends[c][:]
        for e in list(range(1, no)) + [0]:
            acc = dot(keyt[rows_of(outer(e), i), :], prod[c])
            for d in range(1, ni):
                slot = r1.at[c, d - 1, e]
                remote(slot, slot, s1s.at[c, d - 1, e], s1r.at[c, d - 1, e], device(o, inner(d))).wait_recv()
                acc = acc + r1[c, d - 1, e].astype(F32)
            if e:
                sb[c, e - 1] = acc.astype(BF16)
                copy = remote(
                    sb.at[c, e - 1], r2.at[c, e - 1], s2s.at[c, e - 1], s2r.at[c, e - 1],
                    device(outer(e), i),
                )
                copy.start()
                sends[c].append(copy)
        for e in range(1, no):
            slot = r2.at[c, e - 1]
            remote(slot, slot, s2s.at[c, e - 1], s2r.at[c, e - 1], device(outer(e), i)).wait_recv()
            acc = acc + r2[c, e - 1].astype(F32)
        own = rows_of(o, i)
        sf[buf, c, own] = acc.astype(BF16)
        for e in range(1, no):
            copy = remote(
                sf.at[buf, c, own], sf.at[buf, c, own], g2s.at[c, e - 1], g2r.at[c, e - 1],
                device(outer(e), i),
            )
            copy.start()
            sends[c].append(copy)
        forward(c, buf, 0, own)

    def forward(c, buf, e, rows):
        for d in range(1, ni):
            copy = remote(
                sf.at[buf, c, rows], sf.at[buf, c, rows], g1s.at[c, d - 1, e],
                g1r.at[c, d - 1, e], device(o, inner(d)),
            )
            copy.start()
            sends[c].append(copy)

    def relay(c, buf):
        for e in range(1, no):
            rows = rows_of(outer(no - e), i)
            slot = sf.at[buf, c, rows]
            remote(slot, slot, g2s.at[c, e - 1], g2r.at[c, e - 1], device(outer(e), i)).wait_recv()
            forward(c, buf, e, rows)

    def arrive(c, buf):
        for e in range(no):
            for d in range(1, ni):
                slot = sf.at[buf, c, rows_of(outer(no - e), inner(ni - d))]
                remote(slot, slot, g1s.at[c, d - 1, e], g1r.at[c, d - 1, e], device(o, inner(d))).wait_recv()

    def unnormalised(c, buf):
        @pl.loop(0, tokens // tile)
        def _(s):
            rows = pl.ds(pl.multiple_of(s * tile, tile), tile)
            praw[rows, :] = dot(key_ref[rows, :], sf[buf, c])

    def normalise(c, buf):
        gram = dot(sf[buf, c], sf[buf, c], 0, 0)
        if c:
            cross[...] = dot(fact[0], dot(sf[buf, 0], sf[buf, 1], 0, 0), precision=HIGH)
            gram = gram - dot(cross[...], cross[...], 0, 0, precision=HIGH)
        fact[c] = gram
        inverse_factor(fact.at[c])

        @pl.loop(0, tokens // tile)
        def _(s):
            rows = pl.ds(pl.multiple_of(s * tile, tile), tile)
            x = praw[rows, :]
            if c:
                x = x - dot3(raw[rows, :], cross[...])
            x = dot3(x, fact[c], 1, 1)
            if c == 0:
                raw[rows, :] = x
            prod[c, rows] = x.astype(BF16)

    def regroup(c):
        copies = []
        cs = pl.ds(c * CW, CW)
        mine = pl.ds(pl.multiple_of(me * blk, blk), blk)
        for q in range(1, n):
            to = lax.rem(me + q, n)
            copy = remote(
                prod.at[c, pl.ds(pl.multiple_of(to * blk, blk), blk)], comp.at[c, mine],
                fs.at[c, q - 1], fr.at[c, q - 1], {"pos": to},
            )
            copy.start()
            copies.append(copy)
        return copies

    def finish(c):
        mine = pl.ds(pl.multiple_of(me * blk, blk), blk)
        for q in range(1, n):
            slot = comp.at[c, pl.ds(pl.multiple_of(lax.rem(me + n - q, n) * blk, blk), blk)]
            remote(slot, slot, fs.at[c, q - 1], fr.at[c, q - 1], {"pos": lax.rem(me + q, n)}).wait_recv()
        latent_ref[:, c * CW : (c + 1) * CW] = comp[c]
        latent_ref[mine, c * CW : (c + 1) * CW] = prod[c, mine]

    scale = float(width) ** 0.5

    def write_basis(c, buf):
        @pl.loop(0, width // tile)
        def _(s):
            rows = pl.ds(pl.multiple_of(s * tile, tile), tile)
            if c == 0:
                basis_ref[rows, :CW] = scale * dot3(sf[buf, 0, rows], fact[0], 1, 1)
            else:
                x = sf[buf, 1, rows].astype(F32) - dot3(basis_ref[rows, :CW], cross[...]) * (1.0 / scale)
                basis_ref[rows, CW:] = scale * dot3(x, fact[1], 1, 1)

    send(0)
    send(1)
    copies = []
    for t in range(ITERS):
        buf = (t + 1) % 2
        combine(0, buf)
        combine(1, buf)
        relay(0, buf)
        relay(1, buf)
        for c in range(chunks):
            arrive(c, buf)
            unnormalised(c, buf)
            normalise(c, buf)
            if t < ITERS - 1:
                send(c)
            else:
                copies += regroup(c)
    write_basis(0, buf)
    write_basis(1, buf)
    for c in range(chunks):
        finish(c)
        for copy in sends[c]:
            copy.wait_send()
    for copy in copies:
        copy.wait_send()


def local(n, key_cache, init_basis):
    tokens, width = key_cache.shape
    rank = init_basis.shape[1]
    no = 4 if n % 4 == 0 else 1
    ni = n // no
    sub = width // n
    chunks = rank // CW
    vmem = pl.BlockSpec(memory_space=pltpu.VMEM)
    dma = pltpu.SemaphoreType.DMA
    return pl.pallas_call(
        functools.partial(kernel, n, ni, no),
        out_shape=(
            jax.ShapeDtypeStruct((width, rank), F32),
            jax.ShapeDtypeStruct((tokens, rank), BF16),
        ),
        in_specs=[vmem, vmem],
        out_specs=(vmem, vmem),
        scratch_shapes=[
            pltpu.VMEM((width, tokens), BF16),
            pltpu.VMEM((chunks, tokens, CW), BF16),
            pltpu.VMEM((tokens, CW), F32),
            pltpu.VMEM((tokens, CW), F32),
            pltpu.VMEM((chunks, CW, CW), F32),
            pltpu.VMEM((CW, CW), F32),
            pltpu.VMEM((chunks, width, CW), BF16),
            pltpu.VMEM((chunks, ni - 1, no, sub, CW), BF16),
            pltpu.VMEM((chunks, no - 1, sub, CW), BF16),
            pltpu.VMEM((chunks, no - 1, sub, CW), BF16),
            pltpu.VMEM((2, chunks, width, CW), BF16),
            pltpu.VMEM((chunks, tokens, CW), BF16),
            dma((chunks, ni - 1, no)),
            dma((chunks, ni - 1, no)),
            dma((chunks, no - 1)),
            dma((chunks, no - 1)),
            dma((chunks, no - 1)),
            dma((chunks, no - 1)),
            dma((chunks, ni - 1, no)),
            dma((chunks, ni - 1, no)),
            dma((chunks, n - 1)),
            dma((chunks, n - 1)),
        ],
        compiler_params=pltpu.CompilerParams(
            collective_id=0, has_side_effects=True, vmem_limit_bytes=56 * 2**20
        ),
    )(key_cache, init_basis)


def solution(mesh):
    return jax.shard_map(
        functools.partial(local, mesh.shape["pos"]),
        mesh=mesh,
        in_specs=(P(("grp", "pos"), None), P("grp", None)),
        out_specs=(P("grp", None), P(("grp", "pos"), None)),
        check_vma=False,
    )
```

```python
import functools

import jax
import jax.numpy as jnp
from jax import lax
from jax.experimental import pallas as pl
from jax.experimental.pallas import tpu as pltpu
from jax.sharding import PartitionSpec as P

ITERS = 3
CW = 128
F32 = jnp.float32
BF16 = jnp.bfloat16
HIGH = lax.Precision.HIGHEST


def dot(a, b, ca=1, cb=0, precision=None):
    return lax.dot_general(
        a, b, (((ca,), (cb,)), ((), ())), precision=precision, preferred_element_type=F32
    )


def halves(a):
    high = a.astype(BF16)
    return high, (a - high.astype(F32)).astype(BF16)


def dot3(a, b, ca=1, cb=0):
    bh, bl = halves(b)
    if a.dtype == BF16:
        return dot(a, bh, ca, cb) + dot(a, bl, ca, cb)
    ah, al = halves(a)
    return dot(ah, bh, ca, cb) + (dot(ah, bl, ca, cb) + dot(al, bh, ca, cb))


def eliminate(a_ref, low, high):
    sub = lax.broadcasted_iota(jnp.int32, (8, CW), 0)
    lane = lax.broadcasted_iota(jnp.int32, (8, CW), 1)
    a = a_ref[8 * low :, :]
    for k in range(low, high):
        start = 8 * k
        x, rest = a[:8], a[8:]
        left = CW - start - 8
        c = [jnp.broadcast_to(x[:, start + r : start + r + 1], (8, CW)) for r in range(8)]
        inside = (lane >= start) & (lane < start + 8)
        x = jnp.where(inside, jnp.where(lane == start + sub, 1.0, 0.0), x)
        if left:
            g = [jnp.broadcast_to(rest[:, start + r : start + r + 1], (left, CW)) for r in range(8)]
            col = lax.broadcasted_iota(jnp.int32, (left, CW), 1)
            rest = jnp.where((col >= start) & (col < start + 8), 0.0, rest)
        for r in range(8):
            p = lax.rsqrt(c[r][r : r + 1, :])
            row = x[r : r + 1, :] * p
            m = jnp.where(sub > r, c[r] * p, 0.0)
            x = jnp.where(sub == r, row, x - m * row)
            if left:
                gm = g[r] * p
                rest = rest - gm * row
            for t in range(r + 1, 8):
                u = c[t][r : r + 1, :] * p
                c[t] = c[t] - m * u
                if left:
                    g[t] = g[t] - gm * u
        a_ref[start : start + 8, :] = x
        a = rest
    if high < CW // 8:
        a_ref[8 * high :, :] = a
    else:
        rows = lax.broadcasted_iota(jnp.int32, (CW, CW), 0)
        cols = lax.broadcasted_iota(jnp.int32, (CW, CW), 1)
        a_ref[...] = jnp.where(cols <= rows, a_ref[...], 0.0)


def kernel(
    n, ni, no, key_ref, init_ref, basis_ref, latent_ref,
    own_sum, keyt, prod, raw, praw, fact, cross, sl, r1, sb, r2, sf, comp,
    s1s, s1r, s2s, s2r, g2s, g2r, g1s, g1r, fs, fr,
):
    tokens, width = key_ref.shape
    chunks = init_ref.shape[1] // CW
    part, sub, blk = width // ni, width // n, tokens // n
    me = lax.axis_index("pos")
    i, o = lax.rem(me, ni), lax.div(me, ni)

    def device(oo, ii):
        return {"pos": oo * ni + ii}

    def inner(d):
        return lax.rem(i + d, ni)

    def outer(e):
        return lax.rem(o + e, no)

    def rows_of(oo, ii):
        return pl.ds(pl.multiple_of(ii * part + oo * sub, sub), sub)

    def remote(src, dst, ssem, rsem, dev):
        return pltpu.make_async_remote_copy(
            src_ref=src, dst_ref=dst, send_sem=ssem, recv_sem=rsem,
            device_id=dev, device_id_type=pl.DeviceIdType.MESH,
        )

    barrier = pltpu.get_barrier_semaphore()
    for q in range(1, n):
        pl.semaphore_signal(
            barrier, inc=1, device_id={"pos": lax.rem(me + q, n)},
            device_id_type=pl.DeviceIdType.MESH,
        )

    tile = 256

    @pl.loop(0, width // tile)
    def _(s):
        rows = pl.ds(pl.multiple_of(s * tile, tile), tile)
        keyt[rows, :] = key_ref[:, rows].T

    def first(c):
        sf[0, c] = init_ref[:, c * CW : (c + 1) * CW].astype(BF16)

        @pl.loop(0, tokens // tile)
        def _(s):
            rows = pl.ds(pl.multiple_of(s * tile, tile), tile)
            prod[c, rows] = dot(key_ref[rows, :], sf[0, c]).astype(BF16)

    sends = [[] for _ in range(chunks)]

    def send(c):
        for copy in sends[c]:
            copy.wait_send()
        sends[c] = []
        for e in list(range(1, no)) + [0]:
            for d in range(1, ni):
                rows = rows_of(outer(e), inner(d))
                sl[c, rows] = dot(keyt[rows, :], prod[c]).astype(BF16)
                copy = remote(
                    sl.at[c, rows], r1.at[c, d - 1, e], s1s.at[c, d - 1, e],
                    s1r.at[c, d - 1, e], device(o, inner(d)),
                )
                copy.start()
                sends[c].append(copy)

    def reduce(c):
        for e in list(range(1, no)) + [0]:
            acc = dot(keyt[rows_of(outer(e), i), :], prod[c])
            for d in range(1, ni):
                slot = r1.at[c, d - 1, e]
                remote(slot, slot, s1s.at[c, d - 1, e], s1r.at[c, d - 1, e], device(o, inner(d))).wait_recv()
                acc = acc + r1[c, d - 1, e].astype(F32)
            if e:
                sb[c, e - 1] = acc.astype(BF16)
                copy = remote(
                    sb.at[c, e - 1], r2.at[c, e - 1], s2s.at[c, e - 1], s2r.at[c, e - 1],
                    device(outer(e), i),
                )
                copy.start()
                sends[c].append(copy)
            else:
                own_sum[c] = acc

    def total(c, buf):
        acc = own_sum[c]
        for e in range(1, no):
            slot = r2.at[c, e - 1]
            remote(slot, slot, s2s.at[c, e - 1], s2r.at[c, e - 1], device(outer(e), i)).wait_recv()
            acc = acc + r2[c, e - 1].astype(F32)
        own = rows_of(o, i)
        sf[buf, c, own] = acc.astype(BF16)
        for e in range(1, no):
            copy = remote(
                sf.at[buf, c, own], sf.at[buf, c, own], g2s.at[c, e - 1], g2r.at[c, e - 1],
                device(outer(e), i),
            )
            copy.start()
            sends[c].append(copy)
        forward(c, buf, 0, own)

    def forward(c, buf, e, rows):
        for d in range(1, ni):
            copy = remote(
                sf.at[buf, c, rows], sf.at[buf, c, rows], g1s.at[c, d - 1, e],
                g1r.at[c, d - 1, e], device(o, inner(d)),
            )
            copy.start()
            sends[c].append(copy)

    def relay(c, buf):
        for e in range(1, no):
            rows = rows_of(outer(no - e), i)
            slot = sf.at[buf, c, rows]
            remote(slot, slot, g2s.at[c, e - 1], g2r.at[c, e - 1], device(outer(e), i)).wait_recv()
            forward(c, buf, e, rows)

    def arrive(c, buf):
        for e in range(no):
            for d in range(1, ni):
                slot = sf.at[buf, c, rows_of(outer(no - e), inner(ni - d))]
                remote(slot, slot, g1s.at[c, d - 1, e], g1r.at[c, d - 1, e], device(o, inner(d))).wait_recv()

    def unnormalised(c, buf):
        @pl.loop(0, tokens // tile)
        def _(s):
            rows = pl.ds(pl.multiple_of(s * tile, tile), tile)
            praw[rows, :] = dot(key_ref[rows, :], sf[buf, c])

    def gram(c, buf):
        g = dot(sf[buf, c], sf[buf, c], 0, 0)
        if c:
            cross[...] = dot(fact[0], dot(sf[buf, 0], sf[buf, 1], 0, 0), precision=HIGH)
            g = g - dot(cross[...], cross[...], 0, 0, precision=HIGH)
        fact[c] = g

    def project(c):
        @pl.loop(0, tokens // tile)
        def _(s):
            rows = pl.ds(pl.multiple_of(s * tile, tile), tile)
            x = praw[rows, :]
            if c:
                x = x - dot3(raw[rows, :], cross[...])
            x = dot3(x, fact[c], 1, 1)
            if c == 0:
                raw[rows, :] = x
            prod[c, rows] = x.astype(BF16)

    def regroup(c):
        copies = []
        cs = pl.ds(c * CW, CW)
        mine = pl.ds(pl.multiple_of(me * blk, blk), blk)
        for q in range(1, n):
            to = lax.rem(me + q, n)
            copy = remote(
                prod.at[c, pl.ds(pl.multiple_of(to * blk, blk), blk)], comp.at[c, mine],
                fs.at[c, q - 1], fr.at[c, q - 1], {"pos": to},
            )
            copy.start()
            copies.append(copy)
        return copies

    def finish(c):
        mine = pl.ds(pl.multiple_of(me * blk, blk), blk)
        for q in range(1, n):
            slot = comp.at[c, pl.ds(pl.multiple_of(lax.rem(me + n - q, n) * blk, blk), blk)]
            remote(slot, slot, fs.at[c, q - 1], fr.at[c, q - 1], {"pos": lax.rem(me + q, n)}).wait_recv()
        latent_ref[:, c * CW : (c + 1) * CW] = comp[c]
        latent_ref[mine, c * CW : (c + 1) * CW] = prod[c, mine]

    scale = float(width) ** 0.5

    def write_basis(c, buf):
        @pl.loop(0, width // tile)
        def _(s):
            rows = pl.ds(pl.multiple_of(s * tile, tile), tile)
            if c == 0:
                basis_ref[rows, :CW] = scale * dot3(sf[buf, 0, rows], fact[0], 1, 1)
            else:
                x = sf[buf, 1, rows].astype(F32) - dot3(basis_ref[rows, :CW], cross[...]) * (1.0 / scale)
                basis_ref[rows, CW:] = scale * dot3(x, fact[1], 1, 1)

    first(0)
    pl.semaphore_wait(barrier, n - 1)
    send(0)
    first(1)
    send(1)
    reduce(0)
    total(0, 1)
    reduce(1)
    relay(0, 1)
    copies = []
    half = CW // 16
    for t in range(ITERS):
        buf = (t + 1) % 2
        last = t == ITERS - 1
        for c in range(chunks):
            arrive(c, buf)
            unnormalised(c, buf)
            gram(c, buf)
            eliminate(fact.at[c], 0, half)
            if c == 0:
                total(1, buf)
            elif not last:
                total(0, 1 - buf)
            eliminate(fact.at[c], half, 2 * half)
            project(c)
            if last:
                copies += regroup(c)
            else:
                send(c)
            if c == 0:
                relay(1, buf)
            elif not last:
                relay(0, 1 - buf)
            if last:
                write_basis(c, buf)
            else:
                reduce(c)
    for c in range(chunks):
        finish(c)
        for copy in sends[c]:
            copy.wait_send()
    for copy in copies:
        copy.wait_send()


def local(n, key_cache, init_basis):
    tokens, width = key_cache.shape
    rank = init_basis.shape[1]
    no = 4 if n % 4 == 0 else 1
    ni = n // no
    sub = width // n
    chunks = rank // CW
    vmem = pl.BlockSpec(memory_space=pltpu.VMEM)
    dma = pltpu.SemaphoreType.DMA
    return pl.pallas_call(
        functools.partial(kernel, n, ni, no),
        out_shape=(
            jax.ShapeDtypeStruct((width, rank), F32),
            jax.ShapeDtypeStruct((tokens, rank), BF16),
        ),
        in_specs=[vmem, vmem],
        out_specs=(vmem, vmem),
        scratch_shapes=[
            pltpu.VMEM((chunks, sub, CW), F32),
            pltpu.VMEM((width, tokens), BF16),
            pltpu.VMEM((chunks, tokens, CW), BF16),
            pltpu.VMEM((tokens, CW), F32),
            pltpu.VMEM((tokens, CW), F32),
            pltpu.VMEM((chunks, CW, CW), F32),
            pltpu.VMEM((CW, CW), F32),
            pltpu.VMEM((chunks, width, CW), BF16),
            pltpu.VMEM((chunks, ni - 1, no, sub, CW), BF16),
            pltpu.VMEM((chunks, no - 1, sub, CW), BF16),
            pltpu.VMEM((chunks, no - 1, sub, CW), BF16),
            pltpu.VMEM((2, chunks, width, CW), BF16),
            pltpu.VMEM((chunks, tokens, CW), BF16),
            dma((chunks, ni - 1, no)),
            dma((chunks, ni - 1, no)),
            dma((chunks, no - 1)),
            dma((chunks, no - 1)),
            dma((chunks, no - 1)),
            dma((chunks, no - 1)),
            dma((chunks, ni - 1, no)),
            dma((chunks, ni - 1, no)),
            dma((chunks, n - 1)),
            dma((chunks, n - 1)),
        ],
        compiler_params=pltpu.CompilerParams(
            collective_id=0, has_side_effects=True, vmem_limit_bytes=56 * 2**20
        ),
    )(key_cache, init_basis)


def solution(mesh):
    return jax.shard_map(
        functools.partial(local, mesh.shape["pos"]),
        mesh=mesh,
        in_specs=(P(("grp", "pos"), None), P("grp", None)),
        out_specs=(P("grp", None), P(("grp", "pos"), None)),
        check_vma=False,
    )
```

```python
import functools

import jax
import jax.numpy as jnp
from jax import lax
from jax.experimental import pallas as pl
from jax.experimental.pallas import tpu as pltpu
from jax.sharding import PartitionSpec as P

ITERS = 3
CW = 128
F32 = jnp.float32
BF16 = jnp.bfloat16
HIGH = lax.Precision.HIGHEST


def dot(a, b, ca=1, cb=0, precision=None):
    return lax.dot_general(
        a, b, (((ca,), (cb,)), ((), ())), precision=precision, preferred_element_type=F32
    )


def halves(a):
    high = a.astype(BF16)
    return high, (a - high.astype(F32)).astype(BF16)


def dot3(a, b, ca=1, cb=0):
    bh, bl = halves(b)
    if a.dtype == BF16:
        return dot(a, bh, ca, cb) + dot(a, bl, ca, cb)
    ah, al = halves(a)
    return dot(ah, bh, ca, cb) + (dot(ah, bl, ca, cb) + dot(al, bh, ca, cb))


def eliminate(a_ref, low, high):
    sub = lax.broadcasted_iota(jnp.int32, (8, CW), 0)
    lane = lax.broadcasted_iota(jnp.int32, (8, CW), 1)
    a = a_ref[8 * low :, :]
    for k in range(low, high):
        start = 8 * k
        x, rest = a[:8], a[8:]
        left = CW - start - 8
        c = [jnp.broadcast_to(x[:, start + r : start + r + 1], (8, CW)) for r in range(8)]
        inside = (lane >= start) & (lane < start + 8)
        x = jnp.where(inside, jnp.where(lane == start + sub, 1.0, 0.0), x)
        if left:
            g = [jnp.broadcast_to(rest[:, start + r : start + r + 1], (left, CW)) for r in range(8)]
            col = lax.broadcasted_iota(jnp.int32, (left, CW), 1)
            rest = jnp.where((col >= start) & (col < start + 8), 0.0, rest)
        for r in range(8):
            p = lax.rsqrt(c[r][r : r + 1, :])
            row = x[r : r + 1, :] * p
            m = jnp.where(sub > r, c[r] * p, 0.0)
            x = jnp.where(sub == r, row, x - m * row)
            if left:
                gm = g[r] * p
                rest = rest - gm * row
            for t in range(r + 1, 8):
                u = c[t][r : r + 1, :] * p
                c[t] = c[t] - m * u
                if left:
                    g[t] = g[t] - gm * u
        a_ref[start : start + 8, :] = x
        a = rest
    if high < CW // 8:
        a_ref[8 * high :, :] = a
    else:
        rows = lax.broadcasted_iota(jnp.int32, (CW, CW), 0)
        cols = lax.broadcasted_iota(jnp.int32, (CW, CW), 1)
        a_ref[...] = jnp.where(cols <= rows, a_ref[...], 0.0)


def kernel(
    n, ni, no, key_ref, init_ref, basis_ref, latent_ref,
    own_sum, keyt, prod, raw, praw, fact, cross, sl, r1, sb, r2, sf, comp,
    s1s, s1r, s2s, s2r, g2s, g2r, g1s, g1r, fs, fr,
):
    tokens, width = key_ref.shape
    chunks = init_ref.shape[1] // CW
    part, sub, blk = width // ni, width // n, tokens // n
    me = lax.axis_index("pos")
    i, o = lax.rem(me, ni), lax.div(me, ni)

    def device(oo, ii):
        return {"pos": oo * ni + ii}

    def inner(d):
        return lax.rem(i + d, ni)

    def outer(e):
        return lax.rem(o + e, no)

    def rows_of(oo, ii):
        return pl.ds(pl.multiple_of(ii * part + oo * sub, sub), sub)

    def remote(src, dst, ssem, rsem, dev):
        return pltpu.make_async_remote_copy(
            src_ref=src, dst_ref=dst, send_sem=ssem, recv_sem=rsem,
            device_id=dev, device_id_type=pl.DeviceIdType.MESH,
        )

    barrier = pltpu.get_barrier_semaphore()
    for q in range(1, n):
        pl.semaphore_signal(
            barrier, inc=1, device_id={"pos": lax.rem(me + q, n)},
            device_id_type=pl.DeviceIdType.MESH,
        )

    tile = 256

    for c in range(chunks):
        praw[c] = jnp.zeros((tokens, CW), F32)

    @pl.loop(0, width // tile)
    def _(s):
        rows = pl.ds(pl.multiple_of(s * tile, tile), tile)
        keys = key_ref[:, rows]
        keyt[rows, :] = keys.T
        x = dot(keys, init_ref[rows, :].astype(BF16))
        for c in range(chunks):
            praw[c] += x[:, c * CW : (c + 1) * CW]

    for c in range(chunks):
        prod[c] = praw[c].astype(BF16)

    sends = [[] for _ in range(chunks)]

    def send(c):
        for copy in sends[c]:
            copy.wait_send()
        sends[c] = []
        for e in list(range(1, no)) + [0]:
            for d in range(1, ni):
                rows = rows_of(outer(e), inner(d))
                sl[c, rows] = dot(keyt[rows, :], prod[c]).astype(BF16)
                copy = remote(
                    sl.at[c, rows], r1.at[c, d - 1, e], s1s.at[c, d - 1, e],
                    s1r.at[c, d - 1, e], device(o, inner(d)),
                )
                copy.start()
                sends[c].append(copy)

    def reduce(c):
        for e in list(range(1, no)) + [0]:
            acc = dot(keyt[rows_of(outer(e), i), :], prod[c])
            for d in range(1, ni):
                slot = r1.at[c, d - 1, e]
                remote(slot, slot, s1s.at[c, d - 1, e], s1r.at[c, d - 1, e], device(o, inner(d))).wait_recv()
                acc = acc + r1[c, d - 1, e].astype(F32)
            if e:
                sb[c, e - 1] = acc.astype(BF16)
                copy = remote(
                    sb.at[c, e - 1], r2.at[c, e - 1], s2s.at[c, e - 1], s2r.at[c, e - 1],
                    device(outer(e), i),
                )
                copy.start()
                sends[c].append(copy)
            else:
                own_sum[c] = acc

    def total(c, buf):
        acc = own_sum[c]
        for e in range(1, no):
            slot = r2.at[c, e - 1]
            remote(slot, slot, s2s.at[c, e - 1], s2r.at[c, e - 1], device(outer(e), i)).wait_recv()
            acc = acc + r2[c, e - 1].astype(F32)
        own = rows_of(o, i)
        sf[buf, c, own] = acc.astype(BF16)
        for e in range(1, no):
            copy = remote(
                sf.at[buf, c, own], sf.at[buf, c, own], g2s.at[c, e - 1], g2r.at[c, e - 1],
                device(outer(e), i),
            )
            copy.start()
            sends[c].append(copy)
        forward(c, buf, 0, own)

    def forward(c, buf, e, rows):
        for d in range(1, ni):
            copy = remote(
                sf.at[buf, c, rows], sf.at[buf, c, rows], g1s.at[c, d - 1, e],
                g1r.at[c, d - 1, e], device(o, inner(d)),
            )
            copy.start()
            sends[c].append(copy)

    def relay(c, buf):
        for e in range(1, no):
            rows = rows_of(outer(no - e), i)
            slot = sf.at[buf, c, rows]
            remote(slot, slot, g2s.at[c, e - 1], g2r.at[c, e - 1], device(outer(e), i)).wait_recv()
            forward(c, buf, e, rows)

    def partial(c, buf, d):
        j = inner(ni - d)
        cols = pl.ds(pl.multiple_of(j * part, part), part)

        @pl.loop(0, tokens // tile)
        def _(s):
            rows = pl.ds(pl.multiple_of(s * tile, tile), tile)
            x = dot(key_ref[rows, cols], sf[buf, c, cols])
            praw[c, rows] = x if d == 0 else praw[c, rows] + x

        g = dot(sf[buf, c, cols], sf[buf, c, cols], 0, 0)
        fact[c] = g if d == 0 else fact[c] + g
        if c:
            g = dot(sf[buf, 0, cols], sf[buf, 1, cols], 0, 0)
            cross[...] = g if d == 0 else cross[...] + g

    def arrive(c, buf):
        for d in range(1, ni):
            for e in range(no):
                slot = sf.at[buf, c, rows_of(outer(no - e), inner(ni - d))]
                remote(slot, slot, g1s.at[c, d - 1, e], g1r.at[c, d - 1, e], device(o, inner(d))).wait_recv()
            partial(c, buf, d)

    def schur():
        cross[...] = dot(fact[0], cross[...], precision=HIGH)
        fact[1] = fact[1] - dot(cross[...], cross[...], 0, 0, precision=HIGH)

    def project(c):
        @pl.loop(0, tokens // tile)
        def _(s):
            rows = pl.ds(pl.multiple_of(s * tile, tile), tile)
            x = praw[c, rows]
            if c:
                x = x - dot3(raw[rows, :], cross[...])
            x = dot3(x, fact[c], 1, 1)
            if c == 0:
                raw[rows, :] = x
            prod[c, rows] = x.astype(BF16)

    def regroup(c):
        copies = []
        cs = pl.ds(c * CW, CW)
        mine = pl.ds(pl.multiple_of(me * blk, blk), blk)
        for q in range(1, n):
            to = lax.rem(me + q, n)
            copy = remote(
                prod.at[c, pl.ds(pl.multiple_of(to * blk, blk), blk)], comp.at[c, mine],
                fs.at[c, q - 1], fr.at[c, q - 1], {"pos": to},
            )
            copy.start()
            copies.append(copy)
        return copies

    def finish(c):
        mine = pl.ds(pl.multiple_of(me * blk, blk), blk)
        for q in range(1, n):
            slot = comp.at[c, pl.ds(pl.multiple_of(lax.rem(me + n - q, n) * blk, blk), blk)]
            remote(slot, slot, fs.at[c, q - 1], fr.at[c, q - 1], {"pos": lax.rem(me + q, n)}).wait_recv()
        comp[c, mine] = prod[c, mine]
        if c == 0:
            latent_ref[:, :CW] = comp[0]
        else:

            @pl.loop(0, tokens // tile)
            def _(s):
                rows = pl.ds(pl.multiple_of(s * tile, tile), tile)
                x = comp[1, rows].astype(F32) - dot3(comp[0, rows], cross[...])
                latent_ref[rows, CW:] = dot3(x, fact[1], 1, 1).astype(BF16)

    scale = float(width) ** 0.5

    def write_basis(c, buf):
        @pl.loop(0, width // tile)
        def _(s):
            rows = pl.ds(pl.multiple_of(s * tile, tile), tile)
            if c == 0:
                basis_ref[rows, :CW] = scale * dot3(sf[buf, 0, rows], fact[0], 1, 1)
            else:
                x = sf[buf, 1, rows].astype(F32) - dot3(basis_ref[rows, :CW], cross[...]) * (1.0 / scale)
                basis_ref[rows, CW:] = scale * dot3(x, fact[1], 1, 1)

    pl.semaphore_wait(barrier, n - 1)
    send(0)
    send(1)
    reduce(0)
    total(0, 1)
    reduce(1)
    relay(0, 1)
    partial(0, 1, 0)
    copies = []
    half = CW // 16
    for t in range(ITERS):
        buf = (t + 1) % 2
        last = t == ITERS - 1
        arrive(0, buf)
        eliminate(fact.at[0], 0, half)
        total(1, buf)
        eliminate(fact.at[0], half, 2 * half)
        project(0)
        if last:
            copies += regroup(0)
        else:
            send(0)
        relay(1, buf)
        if last:
            write_basis(0, buf)
        else:
            reduce(0)
        partial(1, buf, 0)
        arrive(1, buf)
        if last:
            prod[1] = praw[1].astype(BF16)
            copies += regroup(1)
        schur()
        eliminate(fact.at[1], 0, half)
        if not last:
            total(0, 1 - buf)
        eliminate(fact.at[1], half, 2 * half)
        if last:
            write_basis(1, buf)
        else:
            project(1)
            send(1)
            relay(0, 1 - buf)
            reduce(1)
            partial(0, 1 - buf, 0)
    for c in range(chunks):
        finish(c)
        for copy in sends[c]:
            copy.wait_send()
    for copy in copies:
        copy.wait_send()


def local(n, key_cache, init_basis):
    tokens, width = key_cache.shape
    rank = init_basis.shape[1]
    no = 4 if n % 4 == 0 else 1
    ni = n // no
    sub = width // n
    chunks = rank // CW
    vmem = pl.BlockSpec(memory_space=pltpu.VMEM)
    dma = pltpu.SemaphoreType.DMA
    return pl.pallas_call(
        functools.partial(kernel, n, ni, no),
        out_shape=(
            jax.ShapeDtypeStruct((width, rank), F32),
            jax.ShapeDtypeStruct((tokens, rank), BF16),
        ),
        in_specs=[vmem, vmem],
        out_specs=(vmem, vmem),
        scratch_shapes=[
            pltpu.VMEM((chunks, sub, CW), F32),
            pltpu.VMEM((width, tokens), BF16),
            pltpu.VMEM((chunks, tokens, CW), BF16),
            pltpu.VMEM((tokens, CW), F32),
            pltpu.VMEM((chunks, tokens, CW), F32),
            pltpu.VMEM((chunks, CW, CW), F32),
            pltpu.VMEM((CW, CW), F32),
            pltpu.VMEM((chunks, width, CW), BF16),
            pltpu.VMEM((chunks, ni - 1, no, sub, CW), BF16),
            pltpu.VMEM((chunks, no - 1, sub, CW), BF16),
            pltpu.VMEM((chunks, no - 1, sub, CW), BF16),
            pltpu.VMEM((2, chunks, width, CW), BF16),
            pltpu.VMEM((chunks, tokens, CW), BF16),
            dma((chunks, ni - 1, no)),
            dma((chunks, ni - 1, no)),
            dma((chunks, no - 1)),
            dma((chunks, no - 1)),
            dma((chunks, no - 1)),
            dma((chunks, no - 1)),
            dma((chunks, ni - 1, no)),
            dma((chunks, ni - 1, no)),
            dma((chunks, n - 1)),
            dma((chunks, n - 1)),
        ],
        compiler_params=pltpu.CompilerParams(
            collective_id=0, has_side_effects=True, vmem_limit_bytes=56 * 2**20
        ),
    )(key_cache, init_basis)


def solution(mesh):
    return jax.shard_map(
        functools.partial(local, mesh.shape["pos"]),
        mesh=mesh,
        in_specs=(P(("grp", "pos"), None), P("grp", None)),
        out_specs=(P("grp", None), P(("grp", "pos"), None)),
        check_vma=False,
    )
```

```python
import functools

import jax
import jax.numpy as jnp
from jax import lax
from jax.experimental import pallas as pl
from jax.experimental.pallas import tpu as pltpu
from jax.sharding import PartitionSpec as P

ITERS = 3
CW = 128
F32 = jnp.float32
BF16 = jnp.bfloat16
HIGH = lax.Precision.HIGHEST


def dot(a, b, ca=1, cb=0, precision=None):
    return lax.dot_general(
        a, b, (((ca,), (cb,)), ((), ())), precision=precision, preferred_element_type=F32
    )


def halves(a):
    high = a.astype(BF16)
    return high, (a - high.astype(F32)).astype(BF16)


def dot3(a, b, ca=1, cb=0):
    bh, bl = halves(b)
    if a.dtype == BF16:
        return dot(a, bh, ca, cb) + dot(a, bl, ca, cb)
    ah, al = halves(a)
    return dot(ah, bh, ca, cb) + (dot(ah, bl, ca, cb) + dot(al, bh, ca, cb))


def eliminate(a_ref, low, high):
    sub = lax.broadcasted_iota(jnp.int32, (8, CW), 0)
    lane = lax.broadcasted_iota(jnp.int32, (8, CW), 1)
    a = a_ref[8 * low :, :]
    for k in range(low, high):
        start = 8 * k
        x, rest = a[:8], a[8:]
        left = CW - start - 8
        c = [jnp.broadcast_to(x[:, start + r : start + r + 1], (8, CW)) for r in range(8)]
        inside = (lane >= start) & (lane < start + 8)
        x = jnp.where(inside, jnp.where(lane == start + sub, 1.0, 0.0), x)
        if left:
            g = [jnp.broadcast_to(rest[:, start + r : start + r + 1], (left, CW)) for r in range(8)]
            col = lax.broadcasted_iota(jnp.int32, (left, CW), 1)
            rest = jnp.where((col >= start) & (col < start + 8), 0.0, rest)
        for r in range(8):
            p = lax.rsqrt(c[r][r : r + 1, :])
            row = x[r : r + 1, :] * p
            m = jnp.where(sub > r, c[r] * p, 0.0)
            x = jnp.where(sub == r, row, x - m * row)
            if left:
                gm = g[r] * p
                rest = rest - gm * row
            for t in range(r + 1, 8):
                u = c[t][r : r + 1, :] * p
                c[t] = c[t] - m * u
                if left:
                    g[t] = g[t] - gm * u
        a_ref[start : start + 8, :] = x
        a = rest
    if high < CW // 8:
        a_ref[8 * high :, :] = a
    else:
        rows = lax.broadcasted_iota(jnp.int32, (CW, CW), 0)
        cols = lax.broadcasted_iota(jnp.int32, (CW, CW), 1)
        a_ref[...] = jnp.where(cols <= rows, a_ref[...], 0.0)


def kernel(
    n, ni, no, key_ref, init_ref, basis_ref, latent_ref,
    own_sum, keyt, prod, raw, praw, fact, cross, sl, r1, sb, r2, sf, comp,
    s1s, s1r, s2s, s2r, g2s, g2r, g1s, g1r, fs, fr,
):
    tokens, width = key_ref.shape
    chunks = init_ref.shape[1] // CW
    part, sub, blk = width // ni, width // n, tokens // n
    me = lax.axis_index("pos")
    i, o = lax.rem(me, ni), lax.div(me, ni)

    def device(oo, ii):
        return {"pos": oo * ni + ii}

    def inner(d):
        return lax.rem(i + d, ni)

    def outer(e):
        return lax.rem(o + e, no)

    def rows_of(oo, ii):
        return pl.ds(pl.multiple_of(ii * part + oo * sub, sub), sub)

    def remote(src, dst, ssem, rsem, dev):
        return pltpu.make_async_remote_copy(
            src_ref=src, dst_ref=dst, send_sem=ssem, recv_sem=rsem,
            device_id=dev, device_id_type=pl.DeviceIdType.MESH,
        )

    barrier = pltpu.get_barrier_semaphore()
    for q in range(1, n):
        pl.semaphore_signal(
            barrier, inc=1, device_id={"pos": lax.rem(me + q, n)},
            device_id_type=pl.DeviceIdType.MESH,
        )

    tile = 256

    for c in range(chunks):
        praw[c] = jnp.zeros((tokens, CW), F32)

    @pl.loop(0, width // tile)
    def _(s):
        rows = pl.ds(pl.multiple_of(s * tile, tile), tile)
        keys = key_ref[:, rows]
        keyt[rows, :] = keys.T
        x = dot(keys, init_ref[rows, :].astype(BF16))
        for c in range(chunks):
            praw[c] += x[:, c * CW : (c + 1) * CW]

    for c in range(chunks):
        prod[c] = praw[c].astype(BF16)

    sends = [[] for _ in range(chunks)]

    order = list(range(1, no)) + [0]

    def products(c):
        for copy in sends[c]:
            copy.wait_send()
        sends[c] = []
        for e in order:
            for d in range(1, ni):
                rows = rows_of(outer(e), inner(d))
                sl[c, rows] = dot(keyt[rows, :], prod[c]).astype(BF16)

    def launch(c):
        for e in order:
            for d in range(1, ni):
                copy = remote(
                    sl.at[c, rows_of(outer(e), inner(d))], r1.at[c, d - 1, e],
                    s1s.at[c, d - 1, e], s1r.at[c, d - 1, e], device(o, inner(d)),
                )
                copy.start()
                sends[c].append(copy)

    def reduce(c, e):
        acc = dot(keyt[rows_of(outer(e), i), :], prod[c])
        for d in range(1, ni):
            slot = r1.at[c, d - 1, e]
            remote(slot, slot, s1s.at[c, d - 1, e], s1r.at[c, d - 1, e], device(o, inner(d))).wait_recv()
            acc = acc + r1[c, d - 1, e].astype(F32)
        if e:
            sb[c, e - 1] = acc.astype(BF16)
            copy = remote(
                sb.at[c, e - 1], r2.at[c, e - 1], s2s.at[c, e - 1], s2r.at[c, e - 1],
                device(outer(e), i),
            )
            copy.start()
            sends[c].append(copy)
        else:
            own_sum[c] = acc

    def total(c, buf):
        acc = own_sum[c]
        for e in range(1, no):
            slot = r2.at[c, e - 1]
            remote(slot, slot, s2s.at[c, e - 1], s2r.at[c, e - 1], device(outer(e), i)).wait_recv()
            acc = acc + r2[c, e - 1].astype(F32)
        own = rows_of(o, i)
        sf[buf, c, own] = acc.astype(BF16)
        for e in range(1, no):
            copy = remote(
                sf.at[buf, c, own], sf.at[buf, c, own], g2s.at[c, e - 1], g2r.at[c, e - 1],
                device(outer(e), i),
            )
            copy.start()
            sends[c].append(copy)
        forward(c, buf, 0, own)

    def forward(c, buf, e, rows):
        for d in range(1, ni):
            copy = remote(
                sf.at[buf, c, rows], sf.at[buf, c, rows], g1s.at[c, d - 1, e],
                g1r.at[c, d - 1, e], device(o, inner(d)),
            )
            copy.start()
            sends[c].append(copy)

    def relay(c, buf):
        for e in range(1, no):
            rows = rows_of(outer(no - e), i)
            slot = sf.at[buf, c, rows]
            remote(slot, slot, g2s.at[c, e - 1], g2r.at[c, e - 1], device(outer(e), i)).wait_recv()
            forward(c, buf, e, rows)

    def partial(c, buf, d):
        j = inner(ni - d)
        cols = pl.ds(pl.multiple_of(j * part, part), part)

        @pl.loop(0, tokens // tile)
        def _(s):
            rows = pl.ds(pl.multiple_of(s * tile, tile), tile)
            x = dot(key_ref[rows, cols], sf[buf, c, cols])
            praw[c, rows] = x if d == 0 else praw[c, rows] + x

        g = dot(sf[buf, c, cols], sf[buf, c, cols], 0, 0)
        fact[c] = g if d == 0 else fact[c] + g
        if c:
            g = dot(sf[buf, 0, cols], sf[buf, 1, cols], 0, 0)
            cross[...] = g if d == 0 else cross[...] + g

    def arrive(c, buf):
        for d in range(1, ni):
            for e in range(no):
                slot = sf.at[buf, c, rows_of(outer(no - e), inner(ni - d))]
                remote(slot, slot, g1s.at[c, d - 1, e], g1r.at[c, d - 1, e], device(o, inner(d))).wait_recv()
            partial(c, buf, d)

    def schur():
        cross[...] = dot(fact[0], cross[...], precision=HIGH)
        fact[1] = fact[1] - dot(cross[...], cross[...], 0, 0, precision=HIGH)

    def project(c):
        @pl.loop(0, tokens // tile)
        def _(s):
            rows = pl.ds(pl.multiple_of(s * tile, tile), tile)
            x = praw[c, rows]
            if c:
                x = x - dot3(raw[rows, :], cross[...])
            x = dot3(x, fact[c], 1, 1)
            if c == 0:
                raw[rows, :] = x
            prod[c, rows] = x.astype(BF16)

    def regroup(c):
        copies = []
        cs = pl.ds(c * CW, CW)
        mine = pl.ds(pl.multiple_of(me * blk, blk), blk)
        for q in range(1, n):
            to = lax.rem(me + q, n)
            copy = remote(
                prod.at[c, pl.ds(pl.multiple_of(to * blk, blk), blk)], comp.at[c, mine],
                fs.at[c, q - 1], fr.at[c, q - 1], {"pos": to},
            )
            copy.start()
            copies.append(copy)
        return copies

    def finish(c):
        mine = pl.ds(pl.multiple_of(me * blk, blk), blk)
        for q in range(1, n):
            slot = comp.at[c, pl.ds(pl.multiple_of(lax.rem(me + n - q, n) * blk, blk), blk)]
            remote(slot, slot, fs.at[c, q - 1], fr.at[c, q - 1], {"pos": lax.rem(me + q, n)}).wait_recv()
        comp[c, mine] = prod[c, mine]
        if c == 0:
            latent_ref[:, :CW] = comp[0]
        else:

            @pl.loop(0, tokens // tile)
            def _(s):
                rows = pl.ds(pl.multiple_of(s * tile, tile), tile)
                x = comp[1, rows].astype(F32) - dot3(comp[0, rows], cross[...])
                latent_ref[rows, CW:] = dot3(x, fact[1], 1, 1).astype(BF16)

    scale = float(width) ** 0.5

    def write_basis(c, buf):
        @pl.loop(0, width // tile)
        def _(s):
            rows = pl.ds(pl.multiple_of(s * tile, tile), tile)
            if c == 0:
                basis_ref[rows, :CW] = scale * dot3(sf[buf, 0, rows], fact[0], 1, 1)
            else:
                x = sf[buf, 1, rows].astype(F32) - dot3(basis_ref[rows, :CW], cross[...]) * (1.0 / scale)
                basis_ref[rows, CW:] = scale * dot3(x, fact[1], 1, 1)

    pl.semaphore_wait(barrier, n - 1)
    def factor(c, other, buf):
        steps = CW // 8
        done = 0
        if other is not None:
            for place, e in enumerate(order):
                eliminate(fact.at[c], done, 2 * place + 2)
                done = 2 * place + 2
                reduce(other, e)
        eliminate(fact.at[c], done, steps)
        if other is not None:
            total(other, buf)

    products(0)
    launch(0)
    products(1)
    launch(1)
    for e in order:
        reduce(0, e)
    total(0, 1)
    relay(0, 1)
    partial(0, 1, 0)
    copies = []
    for t in range(ITERS):
        buf = (t + 1) % 2
        last = t == ITERS - 1
        arrive(0, buf)
        factor(0, 1, buf)
        project(0)
        if last:
            relay(1, buf)
            copies += regroup(0)
            write_basis(0, buf)
        else:
            products(0)
            relay(1, buf)
            launch(0)
        partial(1, buf, 0)
        arrive(1, buf)
        if last:
            prod[1] = praw[1].astype(BF16)
            copies += regroup(1)
        schur()
        if last:
            factor(1, None, buf)
            write_basis(1, buf)
        else:
            factor(1, 0, 1 - buf)
            project(1)
            products(1)
            relay(0, 1 - buf)
            launch(1)
            partial(0, 1 - buf, 0)
    for c in range(chunks):
        finish(c)
        for copy in sends[c]:
            copy.wait_send()
    for copy in copies:
        copy.wait_send()


def local(n, key_cache, init_basis):
    tokens, width = key_cache.shape
    rank = init_basis.shape[1]
    no = 4 if n % 4 == 0 else 1
    ni = n // no
    sub = width // n
    chunks = rank // CW
    vmem = pl.BlockSpec(memory_space=pltpu.VMEM)
    dma = pltpu.SemaphoreType.DMA
    return pl.pallas_call(
        functools.partial(kernel, n, ni, no),
        out_shape=(
            jax.ShapeDtypeStruct((width, rank), F32),
            jax.ShapeDtypeStruct((tokens, rank), BF16),
        ),
        in_specs=[vmem, vmem],
        out_specs=(vmem, vmem),
        scratch_shapes=[
            pltpu.VMEM((chunks, sub, CW), F32),
            pltpu.VMEM((width, tokens), BF16),
            pltpu.VMEM((chunks, tokens, CW), BF16),
            pltpu.VMEM((tokens, CW), F32),
            pltpu.VMEM((chunks, tokens, CW), F32),
            pltpu.VMEM((chunks, CW, CW), F32),
            pltpu.VMEM((CW, CW), F32),
            pltpu.VMEM((chunks, width, CW), BF16),
            pltpu.VMEM((chunks, ni - 1, no, sub, CW), BF16),
            pltpu.VMEM((chunks, no - 1, sub, CW), BF16),
            pltpu.VMEM((chunks, no - 1, sub, CW), BF16),
            pltpu.VMEM((2, chunks, width, CW), BF16),
            pltpu.VMEM((chunks, tokens, CW), BF16),
            dma((chunks, ni - 1, no)),
            dma((chunks, ni - 1, no)),
            dma((chunks, no - 1)),
            dma((chunks, no - 1)),
            dma((chunks, no - 1)),
            dma((chunks, no - 1)),
            dma((chunks, ni - 1, no)),
            dma((chunks, ni - 1, no)),
            dma((chunks, n - 1)),
            dma((chunks, n - 1)),
        ],
        compiler_params=pltpu.CompilerParams(
            collective_id=0, has_side_effects=True, vmem_limit_bytes=56 * 2**20
        ),
    )(key_cache, init_basis)


def solution(mesh):
    return jax.shard_map(
        functools.partial(local, mesh.shape["pos"]),
        mesh=mesh,
        in_specs=(P(("grp", "pos"), None), P("grp", None)),
        out_specs=(P("grp", None), P(("grp", "pos"), None)),
        check_vma=False,
    )
```
